32 devices in a mesh: dp: 8 (over z, x), section: 4 (over y, core).
Axes of the slice: x: 2, y: 2, z: 4, core: 2. Of those that a mesh axis runs over, the one named last changes fastest.
Arguments:
- images_in: bfloat16 [2048, 4096], P(('dp', 'section')), may hold values from -6 to 6
- labels: int32 [2048], P(('dp', 'section')), may hold values from 0 to 9
- conv_weight: float32 [3, 2, 576, 64], P(None, None, None, 'section'), may hold values from -0.25 to 0.25
- frn_gain: float32 [3, 2, 64], replicated, may hold values from 0.25 to 1.75
- frn_bias: float32 [3, 2, 64], replicated, may hold values from -3 to 3
- head_weight: float32 [64, 10], replicated, as said below
- head_bias: float32 [10], replicated, may hold values from -4 to 4
Outputs:
- grad_conv: float32 [3, 2, 576, 64], P(None, None, None, 'section')
- grad_norm: float32 [3, 2, 2, 64], replicated
- grad_head_weight: float32 [64, 10], replicated
- grad_head_bias: float32 [10], replicated
The draws below stay inside these ranges and needn't reach their ends.
Inputs may be any that keep to these rules, and one draw needn't show every extreme that they name: `head_weight`: the classifier's weights.
All inputs are finite; a program needn't handle non-finite values.
Results may differ from the reference program's by a relative error of at most 0.0033.
The reference program's roundings to bfloat16 on the way count: a program that leaves them out, or rounds other values in their place, can miss the bound.
Values may be sent and summed in bfloat16 or wider, within the bound.
A program may use at most 64 MiB of HBM per device.

```python
import math
import jax
import jax.numpy as jnp
from jax import lax

C = 64
CLASSES = 10
BLOCKS = 3
SIDE = 8
MICRO = 8
IMG_DEV = 64
PIX = 64
IMAGES = 2048


def draw_head_weight(key, part):
    first = jax.random.fold_in(key, 0)
    base = jnp.clip(jax.random.normal(first, (C, CLASSES), jnp.float32), -4.0, 4.0)
    return base * (2.5 / math.sqrt(C))


def touch_ends(array, own_key, smallest, largest):
    place = [jax.random.randint(jax.random.fold_in(own_key, axis), (), 0, length) for axis, length in enumerate(array.shape)]
    widest = array.shape.index(max(array.shape))
    beside = place[:widest] + [(place[widest] + 1) % array.shape[widest]] + place[widest + 1:]
    return array.at[tuple(place)].set(smallest).at[tuple(beside)].set(largest)


def block_levels(key, shape, shards, least, largest):
    level = 1.0
    for dim, shards_of in shards:
        steps = jax.random.uniform(jax.random.fold_in(jax.random.fold_in(key, 6), dim), (shards_of,), jnp.float32, least / len(shards), largest / len(shards))
        level = level * jnp.repeat(jnp.exp(steps), shape[dim] // shards_of).reshape((-1,) + (1,) * (len(shape) - 1 - dim))
    return level


def scatter_about(rng, dims, scale, bound, cuts=(), held_as=jnp.bfloat16):
    values = jax.random.normal(rng, dims, jnp.float32) * scale
    if len(cuts) > 0:
        values = block_levels(rng, dims, cuts, -0.22, 0.18) * values
    return jnp.clip(values, min=-bound, max=bound).astype(held_as)


def setup_inputs(seed: int = 0) -> dict:
    arg_keys = jax.random.split(jax.random.key(seed), 8)
    return {
        "images_in": scatter_about(arg_keys[0], (IMAGES, PIX * C), 1.0, 6.0, ((0, 32),)),
        "labels": touch_ends(jax.random.randint(arg_keys[1], (IMAGES,), 0, CLASSES), jax.random.fold_in(arg_keys[1], 1), 0, CLASSES - 1).astype(jnp.int32),
        "conv_weight": scatter_about(arg_keys[2], (BLOCKS, 2, 9 * C, C), (9 * C) ** -0.5, 0.25, ((3, 4),), jnp.float32),
        "frn_gain": jnp.clip(1.0 + 0.15 * jax.random.normal(arg_keys[3], (BLOCKS, 2, C), jnp.float32), 0.25, 1.75),
        "frn_bias": scatter_about(arg_keys[4], (BLOCKS, 2, C), 0.5, 3.0, (), jnp.float32),
        "head_weight": draw_head_weight(jax.random.fold_in(arg_keys[7], 71), 0),
        "head_bias": scatter_about(arg_keys[6], (CLASSES,), 1.0, 4.0, (), jnp.float32),
    }


eps = 1e-06
prior_precision = 0.5

def make_patches(maps):
    side = maps.shape[1]
    padded = jnp.pad(maps, ((0, 0), (1, 1), (1, 1), (0, 0)))
    taps = [padded[:, a:a + side, e:e + side, :] for a in range(3) for e in range(3)]
    stacked = jnp.concatenate(taps, axis=3)
    return stacked.reshape(maps.shape[0] * side * side, 9 * maps.shape[3])

def fold_patches(columns, shape):
    back = jax.vjp(make_patches, jnp.zeros(shape, jnp.float32))[1]
    return back(columns)[0]

def respond(values, gain, bias, count):
    grouped = values.reshape(count, -1, values.shape[1])
    energy = lax.optimization_barrier(jnp.mean(grouped * grouped, axis=1, keepdims=True))
    normed = grouped * lax.rsqrt(energy + eps)
    return (gain * normed + bias).reshape(values.shape)

def swish(values):
    return values * jax.nn.sigmoid(values)

def block_forward(maps, weights, gains, biases):
    count = maps.shape[0]
    w_first = weights[0].astype(jnp.bfloat16)
    w_second = weights[1].astype(jnp.bfloat16)
    cols_first = make_patches(maps)
    pre_first = jnp.dot(cols_first, w_first, preferred_element_type=jnp.float32)
    hidden = swish(respond(pre_first, gains[0], biases[0], count)).astype(jnp.bfloat16)
    cols_second = make_patches(hidden.reshape(maps.shape))
    pre_second = jnp.dot(cols_second, w_second, preferred_element_type=jnp.float32)
    skip = maps.reshape(pre_second.shape).astype(jnp.float32)
    result = swish(skip + respond(pre_second, gains[1], biases[1], count)).astype(jnp.bfloat16)
    return (result.reshape(maps.shape), (cols_first, pre_first, cols_second, pre_second))

def block_backward(maps, cotangent, weights, gains, biases):
    count = maps.shape[0]
    w_first = weights[0].astype(jnp.bfloat16)
    w_second = weights[1].astype(jnp.bfloat16)
    saved = block_forward(maps, weights, gains, biases)[1]
    cols_first, pre_first, cols_second, pre_second = saved

    def second_part(values, skip, gain, bias):
        return swish(skip + respond(values, gain, bias, count))

    def first_part(values, gain, bias):
        return swish(respond(values, gain, bias, count))
    skip = maps.reshape(pre_second.shape).astype(jnp.float32)
    back_second = jax.vjp(second_part, pre_second, skip, gains[1], biases[1])[1]
    d_second, d_skip, dg_second, db_second = back_second(cotangent.reshape(pre_second.shape).astype(jnp.float32))
    q_second = d_second.astype(jnp.bfloat16)
    dw_second = jnp.dot(cols_second.T, q_second, preferred_element_type=jnp.float32)
    d_hidden = fold_patches(jnp.dot(q_second, w_second.T, preferred_element_type=jnp.float32), maps.shape)
    back_first = jax.vjp(first_part, pre_first, gains[0], biases[0])[1]
    d_first, dg_first, db_first = back_first(d_hidden.reshape(pre_first.shape))
    q_first = d_first.astype(jnp.bfloat16)
    dw_first = jnp.dot(cols_first.T, q_first, preferred_element_type=jnp.float32)
    d_input = fold_patches(jnp.dot(q_first, w_first.T, preferred_element_type=jnp.float32), maps.shape)
    d_maps = (d_skip.reshape(maps.shape) + d_input).astype(jnp.bfloat16)
    d_norm = jnp.stack([jnp.stack([dg_first, db_first]), jnp.stack([dg_second, db_second])])
    return (d_maps, jnp.stack([dw_first, dw_second]), d_norm)

def head_grads(final, labels, head_w, head_b, total):
    count = final.shape[0]
    width = final.shape[3]
    pixels = final.shape[1] * final.shape[2]
    pooled = lax.optimization_barrier(jnp.mean(final.reshape(count, pixels, width).astype(jnp.float32), axis=1))
    logits = jnp.dot(pooled, head_w, precision=lax.Precision.HIGHEST) + head_b
    top = lax.optimization_barrier(jnp.max(logits, axis=1, keepdims=True))
    expo = jnp.exp(logits - top)
    probs = expo / lax.optimization_barrier(jnp.sum(expo, axis=1, keepdims=True))
    onehot = (labels[:, None] == jnp.arange(head_w.shape[1])[None, :]).astype(jnp.float32)
    d_logits = (probs - onehot) / total
    d_head_w = jnp.dot(pooled.T, d_logits, precision=lax.Precision.HIGHEST)
    d_head_b = lax.optimization_barrier(jnp.sum(d_logits, axis=0))
    d_pooled = jnp.dot(d_logits, head_w.T, precision=lax.Precision.HIGHEST) / pixels
    spread = jnp.broadcast_to(d_pooled[:, None, :], (count, pixels, width))
    return (spread.astype(jnp.bfloat16).reshape(final.shape), d_head_w, d_head_b)

def group_grads(maps, labels, weights, gains, biases, head_w, head_b, total):
    saved = []
    for index in range(weights.shape[0]):
        saved.append(maps)
        maps = block_forward(maps, weights[index], gains[index], biases[index])[0]
    cotangent, d_head_w, d_head_b = head_grads(maps, labels, head_w, head_b, total)
    conv_terms = []
    norm_terms = []
    for index in reversed(range(weights.shape[0])):
        cotangent, d_conv, d_norm = block_backward(saved[index], cotangent, weights[index], gains[index], biases[index])
        conv_terms.insert(0, d_conv)
        norm_terms.insert(0, d_norm)
    return (jnp.stack(conv_terms), jnp.stack(norm_terms), d_head_w, d_head_b)

def accumulate(maps, labels, weights, gains, biases, head_w, head_b, total):
    width = weights.shape[3]
    initial = (jnp.zeros(weights.shape, jnp.float32), jnp.zeros((weights.shape[0], 2, 2, width), jnp.float32), jnp.zeros(head_w.shape, jnp.float32), jnp.zeros(head_b.shape, jnp.float32))

    def advance(carry, item):
        terms = group_grads(item[0], item[1], weights, gains, biases, head_w, head_b, total)
        return (tuple((left + right for left, right in zip(carry, terms))), None)
    return lax.scan(advance, initial, (maps, labels))[0]

def reference(images_in, labels, conv_weight, frn_gain, frn_bias, head_weight, head_bias):
    group_size = IMG_DEV // MICRO
    groups = IMAGES // group_size
    maps = images_in.reshape(groups, group_size, SIDE, SIDE, C)
    label_groups = labels.reshape(groups, group_size)
    conv_sum, norm_sum, head_w_sum, head_b_sum = accumulate(maps, label_groups, conv_weight, frn_gain, frn_bias, head_weight, head_bias, IMAGES)
    params = jnp.stack([frn_gain, frn_bias], axis=2)
    return (conv_sum + prior_precision * conv_weight, norm_sum + prior_precision * params, head_w_sum + prior_precision * head_weight, head_b_sum + prior_precision * head_bias)
```

```python
import functools

import jax
import jax.numpy as jnp
from jax import lax
from jax.experimental import pallas as pl
from jax.experimental.pallas import tpu as pltpu
from jax.sharding import PartitionSpec as P

F32 = jnp.float32
BF16 = jnp.bfloat16
eps = 1e-06
prior_precision = 0.5
OFFSETS = (0, 1, 2, -1)


def kernel(total, img, labels, wt, gain, bias, hw, hb, big, small,
           xs, zs, dsw, rs, wf, wb, qs, qt, du2, du1, hw2, lab):
    lane = lax.broadcasted_iota(jnp.int32, (1, 128), 1)
    low = lane < 64

    def both(v):
        return v + pltpu.roll(v, 64, 1)

    def twice(v):
        return jnp.concatenate([v, v], axis=1)

    for ref in (qs, qt):
        ref[0] = jnp.zeros(ref.shape[1:], BF16)
        ref[9] = jnp.zeros(ref.shape[1:], BF16)
    for k in range(6):
        xs[k, 0] = jnp.zeros((256, 256), BF16)
        xs[k, 9] = jnp.zeros((256, 256), BF16)

    def spread(b, carry):
        flat = wt[b].astype(F32)
        zero = jnp.zeros((64, 128), BF16)
        cols = jnp.concatenate([flat, jnp.zeros((128, 64), F32)], axis=1).T
        plain = [cols[t * 64:(t + 1) * 64] for t in range(9)]
        turned = [pltpu.roll(v, 64, 1) for v in plain]
        none = jnp.zeros((64, 128), F32)
        for j in range(2):
            first, second = (plain, turned) if j == 0 else (turned, plain)
            for a in range(3):
                for s, xi in enumerate(OFFSETS):
                    left = first[a * 3 + xi + 1] if 0 <= xi + 1 <= 2 else none
                    right = second[a * 3 + xi] if 0 <= xi <= 2 else none
                    tile = jnp.where(low, left, right).astype(BF16)
                    for yo in range(2):
                        row = (a + yo) * 256 + s * 64
                        wf[2 * b + j, row:row + 64, yo * 128:yo * 128 + 128] = tile
        wide = jnp.concatenate(
            [jnp.zeros((128, 64), F32), flat, jnp.zeros((128, 128), F32)], axis=1)
        for a in range(3):
            for s, xi in enumerate(OFFSETS):
                at = ((2 - a) * 3 + 2 - xi) * 64
                tile = wide[:, at:at + 128]
                if xi == -1:
                    tile = jnp.where(low, tile, 0.0)
                if xi == 2:
                    tile = jnp.where(low, 0.0, tile)
                tile = tile.astype(BF16)
                for j in range(2):
                    for yo in range(2):
                        row = (a + yo) * 256 + s * 64
                        wb[2 * b + j, row:row + 64, yo * 128:yo * 128 + 128] = (
                            tile[j * 64:j * 64 + 64])
        for j in range(2):
            for ref in (wf, wb):
                for s in range(4):
                    ref[2 * b + j, 768 + s * 64:832 + s * 64, 0:128] = zero
                    ref[2 * b + j, s * 64:s * 64 + 64, 128:256] = zero
        return carry

    lax.fori_loop(0, 3, spread, 0)

    def put(ref, y, v):
        edge = jnp.zeros((1, 64, 128), F32)
        after = jnp.concatenate([v[1:], edge], axis=0)
        before = jnp.concatenate([edge, v[:3]], axis=0)
        beside = jnp.where(low[None], after, before)
        ref[y + 1, :, 0:128] = v.reshape(256, 128).astype(BF16)
        ref[y + 1, :, 128:256] = beside.reshape(256, 128).astype(BF16)

    def conv(src, w, body, init):
        def step(y2, carry):
            rows = jnp.concatenate([src[2 * y2 + r] for r in range(4)], axis=1)
            out = jnp.dot(rows, w[...], preferred_element_type=F32)
            for yo in range(2):
                carry = body(2 * y2 + yo, out[:, yo * 128:yo * 128 + 128], carry)
            return carry
        return lax.fori_loop(0, 4, step, init)

    zero_sum = jnp.zeros((64, 128), F32)

    def over_pairs(v):
        return jnp.sum(v.reshape(4, 64, 128), axis=0)

    for y in range(8):
        slab = jnp.stack([img[:, (y * 4 + j) * 128:(y * 4 + j + 1) * 128]
                          for j in range(4)], axis=0).astype(F32)
        put(xs.at[0], y, slab)

    pooled = zero_sum
    for k in range(6):
        b, j = k // 2, k % 2

        def keep(y, out, energy):
            zs[k, y] = out
            return energy + over_pairs(out * out)

        energy = conv(xs.at[k], wf.at[k], keep, zero_sum)
        r = lax.rsqrt(both(energy) * (1.0 / 64) + eps)
        rs[k] = r
        scale = r * twice(gain[b, j:j + 1, :])
        shift = twice(bias[b, j:j + 1, :])

        def activate(y, carry):
            u = zs[k, y].reshape(4, 64, 128) * scale[None] + shift[None]
            if j == 1:
                u = u + xs[k - 1, y + 1, :, 0:128].astype(F32).reshape(4, 64, 128)
            sig = 0.5 * jnp.tanh(0.5 * u) + 0.5
            out = u * sig
            dsw[k, y] = (sig + out * (1.0 - sig)).reshape(256, 128)
            if k < 5:
                put(xs.at[k + 1], y, out)
                return carry
            return carry + jnp.sum(out.astype(BF16).astype(F32), axis=0)

        pooled = lax.fori_loop(0, 8, activate, pooled)

    pooled = both(pooled) * (1.0 / 64)
    hw2[...] = jnp.zeros((128, 128), F32)
    hw2[0:64, 0:hw.shape[1]] = hw[...]
    hw2[64:128, 0:hw.shape[1]] = hw[...]
    lab[...] = jnp.zeros((8, 128), jnp.int32)
    lab[0:1, 0:64] = labels[...]
    classes = hw.shape[1]
    hbias = jnp.concatenate([hb[...], jnp.zeros((1, 128 - classes), F32)], axis=1)
    logits = jnp.dot(jnp.where(low, pooled, 0.0), hw2[...],
                     precision=lax.Precision.HIGHEST, preferred_element_type=F32) + hbias
    live = lane < classes
    logits = jnp.where(live, logits, -1e30)
    top = jnp.max(logits, axis=1, keepdims=True)
    expo = jnp.where(live, jnp.exp(logits - top), 0.0)
    probs = expo / jnp.sum(expo, axis=1, keepdims=True)
    onehot = jnp.where(
        lax.broadcasted_iota(jnp.int32, (128, 128), 0) == lab[0:1, :], 1.0, 0.0).T
    dl = (probs - onehot[0:64]) * (1.0 / total)
    dlt = jnp.concatenate([dl, jnp.zeros((64, 128), F32)], axis=0).T
    tall = jnp.concatenate([pooled, jnp.zeros((64, 128), F32)], axis=0)
    small[...] = jnp.zeros((32, 128), F32)
    small[16:32, :] = jnp.dot(dlt[0:16], tall, precision=lax.Precision.HIGHEST,
                              preferred_element_type=F32)
    small[12:13, :] = jnp.sum(dl, axis=0, keepdims=True)
    spread_g = lax.dot_general(dl, hw2[...], (((1,), (1,)), ((), ())),
                               precision=lax.Precision.HIGHEST,
                               preferred_element_type=F32) * (1.0 / 64)
    spread_g = spread_g.astype(BF16).astype(F32)

    def tally(k, y, d, sums):
        return (sums[0] + over_pairs(d * zs[k, y]), sums[1] + over_pairs(d))

    def begin(y, sums):
        d = (dsw[5, y].reshape(4, 64, 128) * spread_g[None]).reshape(256, 128)
        du2[y] = d
        return tally(5, y, d, sums)

    sums = lax.fori_loop(0, 8, begin, (zero_sum, zero_sum))
    for k in range(5, -1, -1):
        b, j = k // 2, k % 2
        source = du2 if j == 1 else du1
        r = rs[k]
        dg = both(sums[0]) * r
        db = both(sums[1])
        small[2 * k:2 * k + 1, :] = jnp.sum(dg, axis=0, keepdims=True)
        small[2 * k + 1:2 * k + 2, :] = jnp.sum(db, axis=0, keepdims=True)
        c1 = r * twice(gain[b, j:j + 1, :])
        c2 = c1 * dg * r * (1.0 / 64)

        def settle(y, carry):
            d = (source[y].reshape(4, 64, 128) * c1[None]
                 - zs[k, y].reshape(4, 64, 128) * c2[None])
            if k > 0:
                put(qs, y, d)
            qt[y + 1] = d.reshape(256, 128).T.astype(BF16)
            return carry

        lax.fori_loop(0, 8, settle, 0)

        left = jnp.concatenate(
            [jnp.concatenate([qt[y - a + 2] for y in range(8)], axis=1) for a in range(3)],
            axis=0)
        right = jnp.concatenate([xs[k, y + 1] for y in range(8)], axis=0)
        terms = jnp.dot(left, right, preferred_element_type=F32)
        parts = []
        for a in range(3):
            zero_side = pltpu.roll(terms[a * 128:a * 128 + 64], 64, 1)
            parts.append((zero_side + terms[a * 128 + 64:a * 128 + 128])[:, 0:192])
        big[k] = jnp.concatenate(parts, axis=1)

        if j == 1:
            def to_first(y, out, sums):
                d = out * dsw[k - 1, y]
                du1[y] = d
                return tally(k - 1, y, d, sums)

            sums = conv(qs, wb.at[k], to_first, (zero_sum, zero_sum))
        elif k > 0:
            def to_second(y, out, sums):
                g = (du2[y] + out).astype(BF16).astype(F32)
                d = g * dsw[k - 1, y]
                du2[y] = d
                return tally(k - 1, y, d, sums)

            sums = conv(qs, wb.at[k], to_second, (zero_sum, zero_sum))


def local_grads(total, images_in, labels, wt, gain, bias, hw, hb, interpret=False):
    vmem = pl.BlockSpec(memory_space=pltpu.VMEM)
    return pl.pallas_call(
        functools.partial(kernel, total),
        out_shape=(jax.ShapeDtypeStruct((6, 64, 576), F32),
                   jax.ShapeDtypeStruct((32, 128), F32)),
        in_specs=[vmem] * 7,
        out_specs=(vmem, vmem),
        scratch_shapes=[
            pltpu.VMEM((6, 10, 256, 256), BF16),
            pltpu.VMEM((6, 8, 256, 128), F32),
            pltpu.VMEM((6, 8, 256, 128), F32),
            pltpu.VMEM((6, 64, 128), F32),
            pltpu.VMEM((6, 1024, 256), BF16),
            pltpu.VMEM((6, 1024, 256), BF16),
            pltpu.VMEM((10, 256, 256), BF16),
            pltpu.VMEM((10, 128, 256), BF16),
            pltpu.VMEM((8, 256, 128), F32),
            pltpu.VMEM((8, 256, 128), F32),
            pltpu.VMEM((128, 128), F32),
            pltpu.VMEM((8, 128), jnp.int32),
        ],
        compiler_params=pltpu.CompilerParams(vmem_limit_bytes=52 * 1024 * 1024),
        interpret=interpret,
    )(images_in, labels, wt, gain, bias, hw, hb)


def per_device(images_in, labels, conv_weight, frn_gain, frn_bias, head_weight, head_bias):
    images = images_in.shape[0]
    total = images * lax.axis_size("dp") * lax.axis_size("section")
    share = jnp.swapaxes(conv_weight.astype(BF16), 2, 3)
    wt = lax.all_gather(share, "section", axis=2, tiled=True).reshape(3, 128, 576)
    big, small = local_grads(total, images_in, labels.reshape(1, images), wt, frn_gain,
                             frn_bias, head_weight, head_bias.reshape(1, -1))
    owned = lax.psum_scatter(big, "section", scatter_dimension=1, tiled=True)
    owned = lax.psum(owned, "dp")
    small = lax.psum(small, ("dp", "section"))
    classes = head_bias.shape[0]
    params = jnp.stack([frn_gain, frn_bias], axis=2)
    return (
        jnp.swapaxes(owned, 1, 2).reshape(conv_weight.shape) + prior_precision * conv_weight,
        small[0:12, 0:64].reshape(params.shape) + prior_precision * params,
        small[16:16 + classes, 0:64].T + prior_precision * head_weight,
        small[12, 0:classes] + prior_precision * head_bias,
    )


def solution(mesh):
    return jax.shard_map(
        per_device,
        mesh=mesh,
        in_specs=(
            P(("dp", "section"), None),
            P(("dp", "section")),
            P(None, None, None, "section"),
            P(),
            P(),
            P(),
            P(),
        ),
        out_specs=(P(None, None, None, "section"), P(), P(), P()),
        check_vma=False,
    )
```

```python
import functools

import jax
import jax.numpy as jnp
from jax import lax
from jax.experimental import pallas as pl
from jax.experimental.pallas import tpu as pltpu
from jax.sharding import PartitionSpec as P

F32 = jnp.float32
BF16 = jnp.bfloat16
MESH = pl.DeviceIdType.MESH
eps = 1e-06
prior_precision = 0.5
OFFSETS = (0, 1, 2, -1)


def kernel(total, dps, secs, img, labels, own, gain, bias, hw, hb, conv_out, small,
           xs, zs, dsw, rs, wf, wb, qs, qt, du2, du1, hw2, lab, wt, buf, in_a, tot, in_b,
           fin, w_send, w_recv, a_send, a_recv, b_send, b_recv, c_send, c_recv):
    dp, sec = lax.axis_index("dp"), lax.axis_index("section")
    tiles = in_a.shape[2]
    per = in_b.shape[2]

    barrier = pltpu.get_barrier_semaphore()
    for d in range(1, secs):
        pl.semaphore_signal(barrier, inc=1, device_id=(dp, lax.rem(sec + d, secs)),
                            device_id_type=MESH)

    def greet(d, carry):
        pl.semaphore_signal(barrier, inc=1, device_id=(lax.rem(dp + d, dps), sec),
                            device_id_type=MESH)
        return carry

    lax.fori_loop(1, dps, greet, 0)
    wt[sec] = own[...].astype(BF16)
    pl.semaphore_wait(barrier, secs - 1 + dps - 1)

    def send_w(d):
        return pltpu.make_async_remote_copy(
            src_ref=wt.at[sec], dst_ref=wt.at[sec], send_sem=w_send.at[d - 1],
            recv_sem=w_recv.at[d - 1], device_id=(dp, lax.rem(sec + d, secs)),
            device_id_type=MESH)

    def send_a(b, d):
        to = lax.rem(sec + d, secs)
        return pltpu.make_async_remote_copy(
            src_ref=buf.at[b, to], dst_ref=in_a.at[b, d - 1], send_sem=a_send.at[b, d - 1],
            recv_sem=a_recv.at[b, d - 1], device_id=(dp, to), device_id_type=MESH)

    def send_b(b, d):
        to = lax.rem(dp + d, dps)
        return pltpu.make_async_remote_copy(
            src_ref=tot.at[b, pl.ds(to * per, per)], dst_ref=in_b.at[b, d - 1],
            send_sem=b_send.at[b, d - 1], recv_sem=b_recv.at[b, d - 1],
            device_id=(to, sec), device_id_type=MESH)

    def send_c(b, d):
        to = lax.rem(dp + d, dps)
        mine = fin.at[b, pl.ds(dp * per, per)]
        return pltpu.make_async_remote_copy(
            src_ref=mine, dst_ref=mine, send_sem=c_send.at[b, d - 1],
            recv_sem=c_recv.at[b, d - 1], device_id=(to, sec), device_id_type=MESH)

    def each_dp(act):
        def step(d, carry):
            act(d)
            return carry
        lax.fori_loop(1, dps, step, 0)

    def start_a(b):
        for d in range(1, secs):
            send_a(b, d).start()

    def start_b(b):
        for d in range(1, secs):
            send_a(b, d).wait_recv()
        all_terms = buf[b, sec]
        for d in range(1, secs):
            all_terms = all_terms + in_a[b, d - 1]
        tot[b, 0:tiles] = all_terms
        if tot.shape[1] > tiles:
            tot[b, tiles:] = jnp.zeros((tot.shape[1] - tiles, 8, 128), F32)
        each_dp(lambda d: send_b(b, d).start())

    def start_c(b):
        each_dp(lambda d: send_b(b, d).wait_recv())
        sums = lax.fori_loop(1, dps, lambda d, acc: acc + in_b[b, d - 1],
                             tot[b, pl.ds(dp * per, per)])
        fin[b, pl.ds(dp * per, per)] = sums
        each_dp(lambda d: send_c(b, d).start())

    def end_c(b):
        each_dp(lambda d: send_c(b, d).wait_recv())

    for d in range(1, secs):
        send_w(d).start()
    lane = lax.broadcasted_iota(jnp.int32, (1, 128), 1)
    low = lane < 64

    def both(v):
        return v + pltpu.roll(v, 64, 1)

    def twice(v):
        return jnp.concatenate([v, v], axis=1)

    for ref in (qs, qt):
        ref[0] = jnp.zeros(ref.shape[1:], BF16)
        ref[9] = jnp.zeros(ref.shape[1:], BF16)
    for k in range(6):
        xs[k, 0] = jnp.zeros((256, 256), BF16)
        xs[k, 9] = jnp.zeros((256, 256), BF16)

    def put(ref, y, v):
        edge = jnp.zeros((1, 64, 128), F32)
        after = jnp.concatenate([v[1:], edge], axis=0)
        before = jnp.concatenate([edge, v[:3]], axis=0)
        beside = jnp.where(low[None], after, before)
        ref[y + 1, :, 0:128] = v.reshape(256, 128).astype(BF16)
        ref[y + 1, :, 128:256] = beside.reshape(256, 128).astype(BF16)

    def conv(src, w, body, init):
        def step(y2, carry):
            rows = jnp.concatenate([src[2 * y2 + r] for r in range(4)], axis=1)
            out = jnp.dot(rows, w[...], preferred_element_type=F32)
            for yo in range(2):
                carry = body(2 * y2 + yo, out[:, yo * 128:yo * 128 + 128], carry)
            return carry
        return lax.fori_loop(0, 4, step, init)

    zero_sum = jnp.zeros((64, 128), F32)

    def over_pairs(v):
        return jnp.sum(v.reshape(4, 64, 128), axis=0)

    for y in range(8):
        slab = jnp.stack([img[:, (y * 4 + j) * 128:(y * 4 + j + 1) * 128]
                          for j in range(4)], axis=0).astype(F32)
        put(xs.at[0], y, slab)

    for d in range(1, secs):
        send_w(d).wait_recv()

    def spread(b, carry):
        flat = jnp.concatenate(
            [wt[q, 2 * b + j] for j in range(2) for q in range(secs)], axis=0).astype(F32)
        zero = jnp.zeros((64, 128), BF16)
        cols = jnp.concatenate([flat, jnp.zeros((128, 64), F32)], axis=1).T
        plain = [cols[t * 64:(t + 1) * 64] for t in range(9)]
        turned = [pltpu.roll(v, 64, 1) for v in plain]
        none = jnp.zeros((64, 128), F32)
        for j in range(2):
            first, second = (plain, turned) if j == 0 else (turned, plain)
            for a in range(3):
                for s, xi in enumerate(OFFSETS):
                    left = first[a * 3 + xi + 1] if 0 <= xi + 1 <= 2 else none
                    right = second[a * 3 + xi] if 0 <= xi <= 2 else none
                    tile = jnp.where(low, left, right).astype(BF16)
                    for yo in range(2):
                        row = (a + yo) * 256 + s * 64
                        wf[2 * b + j, row:row + 64, yo * 128:yo * 128 + 128] = tile
        wide = jnp.concatenate(
            [jnp.zeros((128, 64), F32), flat, jnp.zeros((128, 128), F32)], axis=1)
        for a in range(3):
            for s, xi in enumerate(OFFSETS):
                at = ((2 - a) * 3 + 2 - xi) * 64
                tile = wide[:, at:at + 128]
                if xi == -1:
                    tile = jnp.where(low, tile, 0.0)
                if xi == 2:
                    tile = jnp.where(low, 0.0, tile)
                tile = tile.astype(BF16)
                for j in range(2):
                    for yo in range(2):
                        row = (a + yo) * 256 + s * 64
                        wb[2 * b + j, row:row + 64, yo * 128:yo * 128 + 128] = (
                            tile[j * 64:j * 64 + 64])
        for j in range(2):
            for ref in (wf, wb):
                for s in range(4):
                    ref[2 * b + j, 768 + s * 64:832 + s * 64, 0:128] = zero
                    ref[2 * b + j, s * 64:s * 64 + 64, 128:256] = zero
        return carry

    lax.fori_loop(0, 3, spread, 0)

    pooled = zero_sum
    for k in range(6):
        b, j = k // 2, k % 2

        def keep(y, out, energy):
            zs[k, y] = out
            return energy + over_pairs(out * out)

        energy = conv(xs.at[k], wf.at[k], keep, zero_sum)
        r = lax.rsqrt(both(energy) * (1.0 / 64) + eps)
        rs[k] = r
        scale = r * twice(gain[b, j:j + 1, :])
        shift = twice(bias[b, j:j + 1, :])

        def activate(y, carry):
            u = zs[k, y].reshape(4, 64, 128) * scale[None] + shift[None]
            if j == 1:
                u = u + xs[k - 1, y + 1, :, 0:128].astype(F32).reshape(4, 64, 128)
            sig = 0.5 * jnp.tanh(0.5 * u) + 0.5
            out = u * sig
            dsw[k, y] = (sig + out * (1.0 - sig)).reshape(256, 128)
            if k < 5:
                put(xs.at[k + 1], y, out)
                return carry
            return carry + jnp.sum(out.astype(BF16).astype(F32), axis=0)

        pooled = lax.fori_loop(0, 8, activate, pooled)

    pooled = both(pooled) * (1.0 / 64)
    hw2[...] = jnp.zeros((128, 128), F32)
    hw2[0:64, 0:hw.shape[1]] = hw[...]
    hw2[64:128, 0:hw.shape[1]] = hw[...]
    lab[...] = jnp.zeros((8, 128), jnp.int32)
    lab[0:1, 0:64] = labels[...]
    classes = hw.shape[1]
    hbias = jnp.concatenate([hb[...], jnp.zeros((1, 128 - classes), F32)], axis=1)
    logits = jnp.dot(jnp.where(low, pooled, 0.0), hw2[...],
                     precision=lax.Precision.HIGHEST, preferred_element_type=F32) + hbias
    live = lane < classes
    logits = jnp.where(live, logits, -1e30)
    top = jnp.max(logits, axis=1, keepdims=True)
    expo = jnp.where(live, jnp.exp(logits - top), 0.0)
    probs = expo / jnp.sum(expo, axis=1, keepdims=True)
    onehot = jnp.where(
        lax.broadcasted_iota(jnp.int32, (128, 128), 0) == lab[0:1, :], 1.0, 0.0).T
    dl = (probs - onehot[0:64]) * (1.0 / total)
    dlt = jnp.concatenate([dl, jnp.zeros((64, 128), F32)], axis=0).T
    tall = jnp.concatenate([pooled, jnp.zeros((64, 128), F32)], axis=0)
    d_head = jnp.dot(dlt[0:16], tall, precision=lax.Precision.HIGHEST,
                     preferred_element_type=F32)
    row = lax.broadcasted_iota(jnp.int32, (8, 128), 0)
    extra = jnp.where(row == 4, jnp.sum(dl, axis=0, keepdims=True), 0.0)
    for q in range(secs):
        for b in range(3):
            buf[b, q, 19] = d_head[0:8] if b == 2 else jnp.zeros((8, 128), F32)
            buf[b, q, 20] = d_head[8:16] if b == 2 else jnp.zeros((8, 128), F32)
    spread_g = lax.dot_general(dl, hw2[...], (((1,), (1,)), ((), ())),
                               precision=lax.Precision.HIGHEST,
                               preferred_element_type=F32) * (1.0 / 64)
    spread_g = spread_g.astype(BF16).astype(F32)

    def tally(k, y, d, sums):
        return (sums[0] + over_pairs(d * zs[k, y]), sums[1] + over_pairs(d))

    def begin(y, sums):
        d = (dsw[5, y].reshape(4, 64, 128) * spread_g[None]).reshape(256, 128)
        du2[y] = d
        return tally(5, y, d, sums)

    sums = lax.fori_loop(0, 8, begin, (zero_sum, zero_sum))
    for k in range(5, -1, -1):
        b, j = k // 2, k % 2
        source = du2 if j == 1 else du1
        r = rs[k]
        dg = both(sums[0]) * r
        db = both(sums[1])
        extra = jnp.where(row == 2 * j, jnp.sum(dg, axis=0, keepdims=True), extra)
        extra = jnp.where(row == 2 * j + 1, jnp.sum(db, axis=0, keepdims=True), extra)
        if j == 0:
            for q in range(secs):
                buf[b, q, 18] = extra
        c1 = r * twice(gain[b, j:j + 1, :])
        c2 = c1 * dg * r * (1.0 / 64)

        def settle(y, carry):
            d = (source[y].reshape(4, 64, 128) * c1[None]
                 - zs[k, y].reshape(4, 64, 128) * c2[None])
            if k > 0:
                put(qs, y, d)
            qt[y + 1] = d.reshape(256, 128).T.astype(BF16)
            return carry

        lax.fori_loop(0, 8, settle, 0)

        left = jnp.concatenate(
            [jnp.concatenate([qt[y - a + 2] for y in range(8)], axis=1) for a in range(3)],
            axis=0)
        right = jnp.concatenate([xs[k, y + 1] for y in range(8)], axis=0)
        terms = jnp.dot(left, right, preferred_element_type=F32)
        for a in range(3):
            zero_side = pltpu.roll(terms[a * 128:a * 128 + 64], 64, 1)
            both_sides = zero_side + terms[a * 128 + 64:a * 128 + 128]
            for e in range(3):
                at = e // 2 * 128
                here = both_sides[:, at:at + 128]
                there = pltpu.roll(here, 64, 1)
                first, second = (here, there) if e % 2 == 0 else (there, here)
                for q in range(secs):
                    buf[b, q, j * 9 + a * 3 + e] = jnp.where(
                        low, first[q * 16:q * 16 + 8], second[q * 16 + 8:q * 16 + 16])

        if j == 0:
            start_a(b)
        if k <= 3 and j == 1:
            start_b(b + 1)
        if k <= 2 and j == 0:
            start_c(b + 1)

        if j == 1:
            def to_first(y, out, sums):
                d = out * dsw[k - 1, y]
                du1[y] = d
                return tally(k - 1, y, d, sums)

            sums = conv(qs, wb.at[k], to_first, (zero_sum, zero_sum))
        elif k > 0:
            def to_second(y, out, sums):
                g = (du2[y] + out).astype(BF16).astype(F32)
                d = g * dsw[k - 1, y]
                du2[y] = d
                return tally(k - 1, y, d, sums)

            sums = conv(qs, wb.at[k], to_second, (zero_sum, zero_sum))

    start_b(0)
    start_c(0)
    for b in (2, 1, 0):
        end_c(b)
    for b in range(3):
        for j in range(2):
            rows = [fin[b, j * 9 + t] for t in range(9)]
            conv_out[2 * b + j, 0:8] = jnp.concatenate([v[:, 0:64] for v in rows], axis=1)
            conv_out[2 * b + j, 8:16] = jnp.concatenate([v[:, 64:128] for v in rows], axis=1)
        small[b * 8:b * 8 + 8] = fin[b, 18]
    small[24:32] = fin[2, 19]
    small[32:40] = fin[2, 20]
    for d in range(1, secs):
        send_w(d).wait_send()
    for b in range(3):
        for d in range(1, secs):
            send_a(b, d).wait_send()
        each_dp(lambda d: send_b(b, d).wait_send())
        each_dp(lambda d: send_c(b, d).wait_send())


def all_grads(total, dps, secs, images_in, labels, own, gain, bias, hw, hb):
    vmem = pl.BlockSpec(memory_space=pltpu.VMEM)
    tiles = 21
    per = -(-tiles // dps)
    dma = pltpu.SemaphoreType.DMA
    return pl.pallas_call(
        functools.partial(kernel, total, dps, secs),
        out_shape=(jax.ShapeDtypeStruct(own.shape, F32),
                   jax.ShapeDtypeStruct((40, 128), F32)),
        in_specs=[vmem] * 7,
        out_specs=(vmem, vmem),
        scratch_shapes=[
            pltpu.VMEM((6, 10, 256, 256), BF16),
            pltpu.VMEM((6, 8, 256, 128), F32),
            pltpu.VMEM((6, 8, 256, 128), F32),
            pltpu.VMEM((6, 64, 128), F32),
            pltpu.VMEM((6, 1024, 256), BF16),
            pltpu.VMEM((6, 1024, 256), BF16),
            pltpu.VMEM((10, 256, 256), BF16),
            pltpu.VMEM((10, 128, 256), BF16),
            pltpu.VMEM((8, 256, 128), F32),
            pltpu.VMEM((8, 256, 128), F32),
            pltpu.VMEM((128, 128), F32),
            pltpu.VMEM((8, 128), jnp.int32),
            pltpu.VMEM((secs,) + own.shape, BF16),
            pltpu.VMEM((3, secs, tiles, 8, 128), F32),
            pltpu.VMEM((3, secs - 1, tiles, 8, 128), F32),
            pltpu.VMEM((3, per * dps, 8, 128), F32),
            pltpu.VMEM((3, dps - 1, per, 8, 128), F32),
            pltpu.VMEM((3, per * dps, 8, 128), F32),
            dma((secs - 1,)), dma((secs - 1,)),
            dma((3, secs - 1)), dma((3, secs - 1)),
            dma((3, dps - 1)), dma((3, dps - 1)),
            dma((3, dps - 1)), dma((3, dps - 1)),
        ],
        compiler_params=pltpu.CompilerParams(
            vmem_limit_bytes=52 * 1024 * 1024, collective_id=0, has_side_effects=True),
    )(images_in, labels, own, gain, bias, hw, hb)


def per_device(images_in, labels, conv_weight, frn_gain, frn_bias, head_weight, head_bias):
    images = images_in.shape[0]
    dps, secs = lax.axis_size("dp"), lax.axis_size("section")
    blocks, convs, depth, share = conv_weight.shape
    own = jnp.swapaxes(conv_weight, 2, 3).reshape(blocks * convs, share, depth)
    owned, small = all_grads(images * dps * secs, dps, secs, images_in,
                             labels.reshape(1, images), own, frn_gain,
                             frn_bias, head_weight, head_bias.reshape(1, -1))
    classes = head_bias.shape[0]
    params = jnp.stack([frn_gain, frn_bias], axis=2)
    return (
        jnp.swapaxes(owned.reshape(blocks, convs, share, depth), 2, 3)
        + prior_precision * conv_weight,
        small[0:24].reshape(3, 8, 128)[:, 0:4, 0:64].reshape(params.shape)
        + prior_precision * params,
        small[24:24 + classes, 0:64].T + prior_precision * head_weight,
        small[20, 0:classes] + prior_precision * head_bias,
    )


def solution(mesh):
    return jax.shard_map(
        per_device,
        mesh=mesh,
        in_specs=(
            P(("dp", "section"), None),
            P(("dp", "section")),
            P(None, None, None, "section"),
            P(),
            P(),
            P(),
            P(),
        ),
        out_specs=(P(None, None, None, "section"), P(), P(), P()),
        check_vma=False,
    )
```

```python
import functools

import jax
import jax.numpy as jnp
from jax import lax
from jax.experimental import pallas as pl
from jax.experimental.pallas import tpu as pltpu
from jax.sharding import PartitionSpec as P

F32 = jnp.float32
BF16 = jnp.bfloat16
MESH = pl.DeviceIdType.MESH
eps = 1e-06
prior_precision = 0.5
OFFSETS = (0, 1, 2, -1)


CHUNKS = ((5, 4), (3, 2), (1,), (0,))


def chunk_tiles(c):
    return 9 * len(CHUNKS[c]) + (3 if c == 0 else 1)


def kernel(total, dps, secs, img_hbm, labels, own_hbm, gain, bias, hw, hb, conv_out, small,
           xs, zs, dsw, rs, wf, wb, qs, qt, du2, du1, hw2, lab, wt, buf, in_a, tot, in_b,
           fin, img, own, load, w_send, w_recv, a_send, a_recv, b_send, b_recv, c_send, c_recv):
    dp, sec = lax.axis_index("dp"), lax.axis_index("section")
    per = [-(-chunk_tiles(c) // dps) for c in range(len(CHUNKS))]

    load_own = pltpu.make_async_copy(own_hbm, own, load.at[0])
    load_img = pltpu.make_async_copy(img_hbm, img, load.at[1])
    load_own.start()
    load_img.start()
    barrier = pltpu.get_barrier_semaphore()
    for d in range(1, secs):
        pl.semaphore_signal(barrier, inc=1, device_id=(dp, lax.rem(sec + d, secs)),
                            device_id_type=MESH)

    def greet(d, carry):
        pl.semaphore_signal(barrier, inc=1, device_id=(lax.rem(dp + d, dps), sec),
                            device_id_type=MESH)
        return carry

    lax.fori_loop(1, dps, greet, 0)
    load_own.wait()
    wt[sec] = own[...].astype(BF16)
    pl.semaphore_wait(barrier, secs - 1 + dps - 1)

    def send_w(b, d):
        mine = wt.at[sec, pl.ds(2 * b, 2)]
        return pltpu.make_async_remote_copy(
            src_ref=mine, dst_ref=mine, send_sem=w_send.at[b, d - 1],
            recv_sem=w_recv.at[b, d - 1], device_id=(dp, lax.rem(sec + d, secs)),
            device_id_type=MESH)

    def send_a(b, d):
        to = lax.rem(sec + d, secs)
        return pltpu.make_async_remote_copy(
            src_ref=buf.at[b, to, pl.ds(0, chunk_tiles(b))],
            dst_ref=in_a.at[b, d - 1, pl.ds(0, chunk_tiles(b))], send_sem=a_send.at[b, d - 1],
            recv_sem=a_recv.at[b, d - 1], device_id=(dp, to), device_id_type=MESH)

    def send_b(b, d):
        to = lax.rem(dp + d, dps)
        return pltpu.make_async_remote_copy(
            src_ref=tot.at[b, pl.ds(to * per[b], per[b])],
            dst_ref=in_b.at[b, d - 1, pl.ds(0, per[b])],
            send_sem=b_send.at[b, d - 1], recv_sem=b_recv.at[b, d - 1],
            device_id=(to, sec), device_id_type=MESH)

    def send_c(b, d):
        to = lax.rem(dp + d, dps)
        mine = fin.at[b, pl.ds(dp * per[b], per[b])]
        return pltpu.make_async_remote_copy(
            src_ref=mine, dst_ref=mine, send_sem=c_send.at[b, d - 1],
            recv_sem=c_recv.at[b, d - 1], device_id=(to, sec), device_id_type=MESH)

    def each_dp(act):
        def step(d, carry):
            act(d)
            return carry
        lax.fori_loop(1, dps, step, 0)

    def start_a(b):
        for d in range(1, secs):
            send_a(b, d).start()

    def start_b(b):
        for d in range(1, secs):
            send_a(b, d).wait_recv()
        tiles = chunk_tiles(b)
        all_terms = buf[b, sec, 0:tiles]
        for d in range(1, secs):
            all_terms = all_terms + in_a[b, d - 1, 0:tiles]
        tot[b, 0:tiles] = all_terms
        if tot.shape[1] > tiles:
            tot[b, tiles:] = jnp.zeros((tot.shape[1] - tiles, 8, 128), F32)
        each_dp(lambda d: send_b(b, d).start())

    def start_c(b):
        each_dp(lambda d: send_b(b, d).wait_recv())
        sums = lax.fori_loop(1, dps, lambda d, acc: acc + in_b[b, d - 1, 0:per[b]],
                             tot[b, pl.ds(dp * per[b], per[b])])
        fin[b, pl.ds(dp * per[b], per[b])] = sums
        each_dp(lambda d: send_c(b, d).start())

    def end_c(b):
        each_dp(lambda d: send_c(b, d).wait_recv())

    for b in range(3):
        for d in range(1, secs):
            send_w(b, d).start()
    lane = lax.broadcasted_iota(jnp.int32, (1, 128), 1)
    low = lane < 64

    def both(v):
        return v + pltpu.roll(v, 64, 1)

    def twice(v):
        return jnp.concatenate([v, v], axis=1)

    for ref in (qs, qt):
        ref[0] = jnp.zeros(ref.shape[1:], BF16)
        ref[9] = jnp.zeros(ref.shape[1:], BF16)
    for k in range(6):
        xs[k, 0] = jnp.zeros((256, 256), BF16)
        xs[k, 9] = jnp.zeros((256, 256), BF16)

    def put(ref, y, v):
        edge = jnp.zeros((1, 64, 128), F32)
        after = jnp.concatenate([v[1:], edge], axis=0)
        before = jnp.concatenate([edge, v[:3]], axis=0)
        beside = jnp.where(low[None], after, before)
        ref[y + 1, :, 0:128] = v.reshape(256, 128).astype(BF16)
        ref[y + 1, :, 128:256] = beside.reshape(256, 128).astype(BF16)

    def conv(src, w, body, init):
        def step(y2, carry):
            rows = jnp.concatenate([src[2 * y2 + r] for r in range(4)], axis=1)
            out = jnp.dot(rows, w[...], preferred_element_type=F32)
            for yo in range(2):
                carry = body(2 * y2 + yo, out[:, yo * 128:yo * 128 + 128], carry)
            return carry
        return lax.fori_loop(0, 4, step, init)

    zero_sum = jnp.zeros((64, 128), F32)

    def over_pairs(v):
        return jnp.sum(v.reshape(4, 64, 128), axis=0)

    load_img.wait()
    for y in range(8):
        slab = jnp.stack([img[:, (y * 4 + j) * 128:(y * 4 + j + 1) * 128]
                          for j in range(4)], axis=0).astype(F32)
        put(xs.at[0], y, slab)

    def spread(b):
        for d in range(1, secs):
            send_w(b, d).wait_recv()
        flat = jnp.concatenate(
            [wt[q, 2 * b + j] for j in range(2) for q in range(secs)], axis=0).astype(F32)
        zero = jnp.zeros((64, 128), BF16)
        cols = jnp.concatenate([flat, jnp.zeros((128, 64), F32)], axis=1).T
        plain = [cols[t * 64:(t + 1) * 64] for t in range(9)]
        turned = [pltpu.roll(v, 64, 1) for v in plain]
        none = jnp.zeros((64, 128), F32)
        for j in range(2):
            first, second = (plain, turned) if j == 0 else (turned, plain)
            for a in range(3):
                for s, xi in enumerate(OFFSETS):
                    left = first[a * 3 + xi + 1] if 0 <= xi + 1 <= 2 else none
                    right = second[a * 3 + xi] if 0 <= xi <= 2 else none
                    tile = jnp.where(low, left, right).astype(BF16)
                    for yo in range(2):
                        row = (a + yo) * 256 + s * 64
                        wf[2 * b + j, row:row + 64, yo * 128:yo * 128 + 128] = tile
        wide = jnp.concatenate(
            [jnp.zeros((128, 64), F32), flat, jnp.zeros((128, 128), F32)], axis=1)
        for a in range(3):
            for s, xi in enumerate(OFFSETS):
                at = ((2 - a) * 3 + 2 - xi) * 64
                tile = wide[:, at:at + 128]
                if xi == -1:
                    tile = jnp.where(low, tile, 0.0)
                if xi == 2:
                    tile = jnp.where(low, 0.0, tile)
                tile = tile.astype(BF16)
                for j in range(2):
                    for yo in range(2):
                        row = (a + yo) * 256 + s * 64
                        wb[2 * b + j, row:row + 64, yo * 128:yo * 128 + 128] = (
                            tile[j * 64:j * 64 + 64])
        for j in range(2):
            for ref in (wf, wb):
                for s in range(4):
                    ref[2 * b + j, 768 + s * 64:832 + s * 64, 0:128] = zero
                    ref[2 * b + j, s * 64:s * 64 + 64, 128:256] = zero

    pooled = zero_sum
    for k in range(6):
        b, j = k // 2, k % 2
        if j == 0:
            spread(b)

        def keep(y, out, energy):
            zs[k, y] = out
            return energy + over_pairs(out * out)

        energy = conv(xs.at[k], wf.at[k], keep, zero_sum)
        r = lax.rsqrt(both(energy) * (1.0 / 64) + eps)
        rs[k] = r
        scale = r * twice(gain[b, j:j + 1, :])
        shift = twice(bias[b, j:j + 1, :])

        def activate(y, carry):
            u = zs[k, y].reshape(4, 64, 128) * scale[None] + shift[None]
            if j == 1:
                u = u + xs[k - 1, y + 1, :, 0:128].astype(F32).reshape(4, 64, 128)
            sig = 0.5 * jnp.tanh(0.5 * u) + 0.5
            out = u * sig
            dsw[k, y] = (sig + out * (1.0 - sig)).reshape(256, 128)
            if k < 5:
                put(xs.at[k + 1], y, out)
                return carry
            return carry + jnp.sum(out.astype(BF16).astype(F32), axis=0)

        pooled = lax.fori_loop(0, 8, activate, pooled)

    pooled = both(pooled) * (1.0 / 64)
    hw2[...] = jnp.zeros((128, 128), F32)
    hw2[0:hw.shape[0], :] = twice(hw[...])
    lab[...] = jnp.zeros((8, 128), jnp.int32)
    lab[0:1, 0:64] = labels[...]
    classes = hw.shape[0]
    hbias = jnp.concatenate([hb[...], jnp.zeros((1, 128 - classes), F32)], axis=1)
    logits = lax.dot_general(jnp.where(low, pooled, 0.0), hw2[...],
                             (((1,), (1,)), ((), ())), precision=lax.Precision.HIGHEST,
                             preferred_element_type=F32) + hbias
    live = lane < classes
    logits = jnp.where(live, logits, -1e30)
    top = jnp.max(logits, axis=1, keepdims=True)
    expo = jnp.where(live, jnp.exp(logits - top), 0.0)
    probs = expo / jnp.sum(expo, axis=1, keepdims=True)
    onehot = jnp.where(
        lax.broadcasted_iota(jnp.int32, (128, 128), 0) == lab[0:1, :], 1.0, 0.0).T
    dl = (probs - onehot[0:64]) * (1.0 / total)
    dlt = jnp.concatenate([dl, jnp.zeros((64, 128), F32)], axis=0).T
    tall = jnp.concatenate([pooled, jnp.zeros((64, 128), F32)], axis=0)
    d_head = jnp.dot(dlt[0:16], tall, precision=lax.Precision.HIGHEST,
                     preferred_element_type=F32)
    row = lax.broadcasted_iota(jnp.int32, (8, 128), 0)
    extra = jnp.where(row == 4, jnp.sum(dl, axis=0, keepdims=True), 0.0)
    for q in range(secs):
        buf[0, q, 19] = d_head[0:8]
        buf[0, q, 20] = d_head[8:16]
    spread_g = jnp.dot(dl, hw2[...], precision=lax.Precision.HIGHEST,
                       preferred_element_type=F32) * (1.0 / 64)
    spread_g = spread_g.astype(BF16).astype(F32)

    def tally(k, y, d, sums):
        return (sums[0] + over_pairs(d * zs[k, y]), sums[1] + over_pairs(d))

    def begin(y, sums):
        d = (dsw[5, y].reshape(4, 64, 128) * spread_g[None]).reshape(256, 128)
        du2[y] = d
        return tally(5, y, d, sums)

    sums = lax.fori_loop(0, 8, begin, (zero_sum, zero_sum))
    for k in range(5, -1, -1):
        b, j = k // 2, k % 2
        source = du2 if j == 1 else du1
        c = [k in ks for ks in CHUNKS].index(True)
        at_tile = CHUNKS[c].index(k)
        ends = k == CHUNKS[c][-1]
        r = rs[k]
        dg = both(sums[0]) * r
        db = both(sums[1])
        extra = jnp.where(row == 2 * at_tile, jnp.sum(dg, axis=0, keepdims=True), extra)
        extra = jnp.where(row == 2 * at_tile + 1, jnp.sum(db, axis=0, keepdims=True), extra)
        if ends:
            for q in range(secs):
                buf[c, q, 9 * len(CHUNKS[c])] = extra
            extra = jnp.zeros((8, 128), F32)
        c1 = r * twice(gain[b, j:j + 1, :])
        c2 = c1 * dg * r * (1.0 / 64)

        def settle(y, carry):
            d = (source[y].reshape(4, 64, 128) * c1[None]
                 - zs[k, y].reshape(4, 64, 128) * c2[None])
            if k > 0:
                put(qs, y, d)
            qt[y + 1] = d.reshape(256, 128).T.astype(BF16)
            return carry

        lax.fori_loop(0, 8, settle, 0)

        left = jnp.concatenate(
            [jnp.concatenate([qt[y - a + 2] for y in range(8)], axis=1) for a in range(3)],
            axis=0)
        right = jnp.concatenate([xs[k, y + 1] for y in range(8)], axis=0)
        terms = jnp.dot(left, right, preferred_element_type=F32)
        for a in range(3):
            zero_side = pltpu.roll(terms[a * 128:a * 128 + 64], 64, 1)
            both_sides = zero_side + terms[a * 128 + 64:a * 128 + 128]
            for e in range(3):
                at = e // 2 * 128
                here = both_sides[:, at:at + 128]
                there = pltpu.roll(here, 64, 1)
                first, second = (here, there) if e % 2 == 0 else (there, here)
                for q in range(secs):
                    buf[c, q, at_tile * 9 + a * 3 + e] = jnp.where(
                        low, first[q * 16:q * 16 + 8], second[q * 16 + 8:q * 16 + 16])

        if ends:
            start_a(c)
        if k == 3:
            start_b(0)
        if k == 2:
            start_c(0)

        if j == 1:
            def to_first(y, out, sums):
                d = out * dsw[k - 1, y]
                du1[y] = d
                return tally(k - 1, y, d, sums)

            sums = conv(qs, wb.at[k], to_first, (zero_sum, zero_sum))
            if k == 1:
                start_b(1)
        elif k > 0:
            def to_second(y, out, sums):
                g = (du2[y] + out).astype(BF16).astype(F32)
                d = g * dsw[k - 1, y]
                du2[y] = d
                return tally(k - 1, y, d, sums)

            sums = conv(qs, wb.at[k], to_second, (zero_sum, zero_sum))

    start_c(1)
    start_b(2)
    start_b(3)
    start_c(2)
    start_c(3)
    for c, ks in enumerate(CHUNKS):
        end_c(c)
        for at_tile, k in enumerate(ks):
            rows = [fin[c, at_tile * 9 + t] for t in range(9)]
            conv_out[k, 0:8] = jnp.concatenate([v[:, 0:64] for v in rows], axis=1)
            conv_out[k, 8:16] = jnp.concatenate([v[:, 64:128] for v in rows], axis=1)
            small[2 * k:2 * k + 2] = fin[c, 9 * len(ks)][2 * at_tile:2 * at_tile + 2]
        if c == 0:
            small[12:13] = fin[c, 18][4:5]
            small[16:24] = fin[c, 19]
            small[24:32] = fin[c, 20]
    for b in range(3):
        for d in range(1, secs):
            send_w(b, d).wait_send()
    for c in range(len(CHUNKS)):
        for d in range(1, secs):
            send_a(c, d).wait_send()
        each_dp(lambda d: send_b(c, d).wait_send())
        each_dp(lambda d: send_c(c, d).wait_send())


def all_grads(total, dps, secs, images_in, labels, own, gain, bias, hw, hb):
    vmem = pl.BlockSpec(memory_space=pltpu.VMEM)
    chunks = len(CHUNKS)
    tiles = max(chunk_tiles(c) for c in range(chunks))
    per = -(-tiles // dps)
    hbm = pl.BlockSpec(memory_space=pltpu.HBM)
    dma = pltpu.SemaphoreType.DMA
    return pl.pallas_call(
        functools.partial(kernel, total, dps, secs),
        out_shape=(jax.ShapeDtypeStruct(own.shape, F32),
                   jax.ShapeDtypeStruct((32, 128), F32)),
        in_specs=[hbm, vmem, hbm, vmem, vmem, vmem, vmem],
        out_specs=(vmem, vmem),
        scratch_shapes=[
            pltpu.VMEM((6, 10, 256, 256), BF16),
            pltpu.VMEM((6, 8, 256, 128), F32),
            pltpu.VMEM((6, 8, 256, 128), F32),
            pltpu.VMEM((6, 64, 128), F32),
            pltpu.VMEM((6, 1024, 256), BF16),
            pltpu.VMEM((6, 1024, 256), BF16),
            pltpu.VMEM((10, 256, 256), BF16),
            pltpu.VMEM((10, 128, 256), BF16),
            pltpu.VMEM((8, 256, 128), F32),
            pltpu.VMEM((8, 256, 128), F32),
            pltpu.VMEM((128, 128), F32),
            pltpu.VMEM((8, 128), jnp.int32),
            pltpu.VMEM((secs,) + own.shape, BF16),
            pltpu.VMEM((chunks, secs, tiles, 8, 128), F32),
            pltpu.VMEM((chunks, secs - 1, tiles, 8, 128), F32),
            pltpu.VMEM((chunks, per * dps, 8, 128), F32),
            pltpu.VMEM((chunks, dps - 1, per, 8, 128), F32),
            pltpu.VMEM((chunks, per * dps, 8, 128), F32),
            pltpu.VMEM(images_in.shape, BF16),
            pltpu.VMEM(own.shape, F32),
            dma((2,)),
            dma((3, secs - 1)), dma((3, secs - 1)),
            dma((chunks, secs - 1)), dma((chunks, secs - 1)),
            dma((chunks, dps - 1)), dma((chunks, dps - 1)),
            dma((chunks, dps - 1)), dma((chunks, dps - 1)),
        ],
        compiler_params=pltpu.CompilerParams(
            vmem_limit_bytes=52 * 1024 * 1024, collective_id=0, has_side_effects=True),
    )(images_in, labels, own, gain, bias, hw, hb)


def per_device(images_in, labels, conv_weight, frn_gain, frn_bias, head_weight, head_bias):
    images = images_in.shape[0]
    dps, secs = lax.axis_size("dp"), lax.axis_size("section")
    blocks, convs, depth, share = conv_weight.shape
    own = jnp.swapaxes(conv_weight, 2, 3).reshape(blocks * convs, share, depth)
    owned, small = all_grads(images * dps * secs, dps, secs, images_in,
                             labels.reshape(1, images), own, frn_gain,
                             frn_bias, head_weight.T, head_bias.reshape(1, -1))
    classes = head_bias.shape[0]
    params = jnp.stack([frn_gain, frn_bias], axis=2)
    return (
        jnp.swapaxes(owned.reshape(blocks, convs, share, depth), 2, 3)
        + prior_precision * conv_weight,
        small[0:12, 0:64].reshape(params.shape)
        + prior_precision * params,
        small[16:16 + classes, 0:64].T + prior_precision * head_weight,
        small[12, 0:classes] + prior_precision * head_bias,
    )


def solution(mesh):
    return jax.shard_map(
        per_device,
        mesh=mesh,
        in_specs=(
            P(("dp", "section"), None),
            P(("dp", "section")),
            P(None, None, None, "section"),
            P(),
            P(),
            P(),
            P(),
        ),
        out_specs=(P(None, None, None, "section"), P(), P(), P()),
        check_vma=False,
    )
```

```python
import functools

import jax
import jax.numpy as jnp
from jax import lax
from jax.experimental import pallas as pl
from jax.experimental.pallas import tpu as pltpu
from jax.sharding import PartitionSpec as P

F32 = jnp.float32
BF16 = jnp.bfloat16
MESH = pl.DeviceIdType.MESH
eps = 1e-06
prior_precision = 0.5
OFFSETS = (0, 1, 2, -1)


CHUNKS = ((5, 4), (3, 2), (1,), (0,))


def chunk_tiles(c):
    return 9 * len(CHUNKS[c]) + (3 if c == 0 else 1)


def kernel(total, dps, secs, img_hbm, labels, own_hbm, gain, bias, hw, hb, conv_out, small,
           xs, zs, dsw, rs, wf, wb, qs, qt, du2, du1, hw2, lab, wt, buf, in_a, tot, in_b,
           fin, img, own, load, w_send, w_recv, a_send, a_recv, b_send, b_recv, c_send, c_recv):
    dp, sec = lax.axis_index("dp"), lax.axis_index("section")
    per = [-(-chunk_tiles(c) // dps) for c in range(len(CHUNKS))]

    load_own = pltpu.make_async_copy(own_hbm, own, load.at[0])
    load_img = pltpu.make_async_copy(img_hbm, img, load.at[1])
    load_own.start()
    load_img.start()
    barrier = pltpu.get_barrier_semaphore()
    for d in range(1, secs):
        pl.semaphore_signal(barrier, inc=1, device_id=(dp, lax.rem(sec + d, secs)),
                            device_id_type=MESH)

    def greet(d, carry):
        pl.semaphore_signal(barrier, inc=1, device_id=(lax.rem(dp + d, dps), sec),
                            device_id_type=MESH)
        return carry

    lax.fori_loop(1, dps, greet, 0)
    load_own.wait()
    wt[sec] = own[...].astype(BF16)
    pl.semaphore_wait(barrier, secs - 1 + dps - 1)

    def send_w(b, d):
        mine = wt.at[sec, pl.ds(2 * b, 2)]
        return pltpu.make_async_remote_copy(
            src_ref=mine, dst_ref=mine, send_sem=w_send.at[b, d - 1],
            recv_sem=w_recv.at[b, d - 1], device_id=(dp, lax.rem(sec + d, secs)),
            device_id_type=MESH)

    def send_a(b, d):
        to = lax.rem(sec + d, secs)
        return pltpu.make_async_remote_copy(
            src_ref=buf.at[b, to, pl.ds(0, chunk_tiles(b))],
            dst_ref=in_a.at[b, d - 1, pl.ds(0, chunk_tiles(b))], send_sem=a_send.at[b, d - 1],
            recv_sem=a_recv.at[b, d - 1], device_id=(dp, to), device_id_type=MESH)

    def send_b(b, d):
        to = lax.rem(dp + d, dps)
        return pltpu.make_async_remote_copy(
            src_ref=tot.at[b, pl.ds(to * per[b], per[b])],
            dst_ref=in_b.at[b, d - 1, pl.ds(0, per[b])],
            send_sem=b_send.at[b, d - 1], recv_sem=b_recv.at[b, d - 1],
            device_id=(to, sec), device_id_type=MESH)

    def send_c(b, d):
        to = lax.rem(dp + d, dps)
        mine = fin.at[b, pl.ds(dp * per[b], per[b])]
        return pltpu.make_async_remote_copy(
            src_ref=mine, dst_ref=mine, send_sem=c_send.at[b, d - 1],
            recv_sem=c_recv.at[b, d - 1], device_id=(to, sec), device_id_type=MESH)

    def each_dp(act):
        def step(d, carry):
            act(d)
            return carry
        lax.fori_loop(1, dps, step, 0)

    def start_a(b):
        for d in range(1, secs):
            send_a(b, d).start()

    def start_b(b):
        for d in range(1, secs):
            send_a(b, d).wait_recv()
        tiles = chunk_tiles(b)
        all_terms = buf[b, sec, 0:tiles]
        for d in range(1, secs):
            all_terms = all_terms + in_a[b, d - 1, 0:tiles]
        tot[b, 0:tiles] = all_terms
        if tot.shape[1] > tiles:
            tot[b, tiles:] = jnp.zeros((tot.shape[1] - tiles, 8, 128), F32)
        each_dp(lambda d: send_b(b, d).start())

    def start_c(b):
        each_dp(lambda d: send_b(b, d).wait_recv())
        sums = lax.fori_loop(1, dps, lambda d, acc: acc + in_b[b, d - 1, 0:per[b]],
                             tot[b, pl.ds(dp * per[b], per[b])])
        fin[b, pl.ds(dp * per[b], per[b])] = sums
        each_dp(lambda d: send_c(b, d).start())

    def end_c(b):
        each_dp(lambda d: send_c(b, d).wait_recv())

    for b in range(3):
        for d in range(1, secs):
            send_w(b, d).start()
    lane = lax.broadcasted_iota(jnp.int32, (1, 128), 1)
    low = lane < 64

    def both(v):
        return v + pltpu.roll(v, 64, 1)

    def twice(v):
        return jnp.concatenate([v, v], axis=1)

    for ref in (qs, qt):
        ref[0] = jnp.zeros(ref.shape[1:], BF16)
        ref[9] = jnp.zeros(ref.shape[1:], BF16)
    for k in range(6):
        xs[k, 0] = jnp.zeros((256, 256), BF16)
        xs[k, 9] = jnp.zeros((256, 256), BF16)

    def put(ref, y, v):
        edge = jnp.zeros((1, 64, 128), F32)
        after = jnp.concatenate([v[1:], edge], axis=0)
        before = jnp.concatenate([edge, v[:3]], axis=0)
        beside = jnp.where(low[None], after, before)
        ref[y + 1, :, 0:128] = v.reshape(256, 128).astype(BF16)
        ref[y + 1, :, 128:256] = beside.reshape(256, 128).astype(BF16)

    def conv(src, w, body, init):
        def step(y2, carry):
            rows = jnp.concatenate([src[2 * y2 + r] for r in range(4)], axis=1)
            out = jnp.dot(rows, w[...], preferred_element_type=F32)
            for yo in range(2):
                carry = body(2 * y2 + yo, out[:, yo * 128:yo * 128 + 128], carry)
            return carry
        return lax.fori_loop(0, 4, step, init)

    zero_sum = jnp.zeros((64, 128), F32)

    def over_pairs(v):
        return jnp.sum(v.reshape(4, 64, 128), axis=0)

    load_img.wait()
    for y in range(8):
        slab = jnp.stack([img[:, (y * 4 + j) * 128:(y * 4 + j + 1) * 128]
                          for j in range(4)], axis=0).astype(F32)
        put(xs.at[0], y, slab)

    def spread(b):
        for d in range(1, secs):
            send_w(b, d).wait_recv()
        flat = jnp.concatenate(
            [wt[q, 2 * b + j] for j in range(2) for q in range(secs)], axis=0).astype(F32)
        zero = jnp.zeros((64, 128), BF16)
        cols = jnp.concatenate([flat, jnp.zeros((128, 64), F32)], axis=1).T
        plain = [cols[t * 64:(t + 1) * 64] for t in range(9)]
        turned = [pltpu.roll(v, 64, 1) for v in plain]
        none = jnp.zeros((64, 128), F32)
        for j in range(2):
            first, second = (plain, turned) if j == 0 else (turned, plain)
            for a in range(3):
                for s, xi in enumerate(OFFSETS):
                    left = first[a * 3 + xi + 1] if 0 <= xi + 1 <= 2 else none
                    right = second[a * 3 + xi] if 0 <= xi <= 2 else none
                    tile = jnp.where(low, left, right).astype(BF16)
                    for yo in range(2):
                        row = (a + yo) * 256 + s * 64
                        wf[2 * b + j, row:row + 64, yo * 128:yo * 128 + 128] = tile
        wide = jnp.concatenate(
            [jnp.zeros((128, 64), F32), flat, jnp.zeros((128, 128), F32)], axis=1)
        for a in range(3):
            for s, xi in enumerate(OFFSETS):
                at = ((2 - a) * 3 + 2 - xi) * 64
                tile = wide[:, at:at + 128]
                if xi == -1:
                    tile = jnp.where(low, tile, 0.0)
                if xi == 2:
                    tile = jnp.where(low, 0.0, tile)
                tile = tile.astype(BF16)
                for j in range(2):
                    for yo in range(2):
                        row = (a + yo) * 256 + s * 64
                        wb[2 * b + j, row:row + 64, yo * 128:yo * 128 + 128] = (
                            tile[j * 64:j * 64 + 64])
        for j in range(2):
            for ref in (wf, wb):
                for s in range(4):
                    ref[2 * b + j, 768 + s * 64:832 + s * 64, 0:128] = zero
                    ref[2 * b + j, s * 64:s * 64 + 64, 128:256] = zero

    pooled = zero_sum
    for k in range(6):
        b, j = k // 2, k % 2
        if j == 0:
            spread(b)

        def keep(y, out, energy):
            zs[k, y] = out
            return energy + over_pairs(out * out)

        energy = conv(xs.at[k], wf.at[k], keep, zero_sum)
        r = lax.rsqrt(both(energy) * (1.0 / 64) + eps)
        rs[k] = r
        scale = r * twice(gain[b, j:j + 1, :])
        shift = twice(bias[b, j:j + 1, :])

        def activate(y, carry):
            u = zs[k, y].reshape(4, 64, 128) * scale[None] + shift[None]
            if j == 1:
                u = u + xs[k - 1, y + 1, :, 0:128].astype(F32).reshape(4, 64, 128)
            sig = 0.5 * jnp.tanh(0.5 * u) + 0.5
            out = u * sig
            dsw[k, y] = (sig + out * (1.0 - sig)).reshape(256, 128)
            if k < 5:
                put(xs.at[k + 1], y, out)
                return carry
            return carry + jnp.sum(out.astype(BF16).astype(F32), axis=0)

        pooled = lax.fori_loop(0, 8, activate, pooled)

    pooled = both(pooled) * (1.0 / 64)
    hw2[...] = jnp.zeros((128, 128), F32)
    hw2[0:hw.shape[0], :] = twice(hw[...])
    lab[...] = jnp.zeros((8, 128), jnp.int32)
    lab[0:1, 0:64] = labels[...]
    classes = hw.shape[0]
    hbias = jnp.concatenate([hb[...], jnp.zeros((1, 128 - classes), F32)], axis=1)
    logits = lax.dot_general(jnp.where(low, pooled, 0.0), hw2[...],
                             (((1,), (1,)), ((), ())), precision=lax.Precision.HIGHEST,
                             preferred_element_type=F32) + hbias
    live = lane < classes
    logits = jnp.where(live, logits, -1e30)
    top = jnp.max(logits, axis=1, keepdims=True)
    expo = jnp.where(live, jnp.exp(logits - top), 0.0)
    probs = expo / jnp.sum(expo, axis=1, keepdims=True)
    onehot = jnp.where(
        lax.broadcasted_iota(jnp.int32, (128, 128), 0) == lab[0:1, :], 1.0, 0.0).T
    dl = (probs - onehot[0:64]) * (1.0 / total)
    dlt = jnp.concatenate([dl, jnp.zeros((64, 128), F32)], axis=0).T
    tall = jnp.concatenate([pooled, jnp.zeros((64, 128), F32)], axis=0)
    d_head = jnp.dot(dlt[0:16], tall, precision=lax.Precision.HIGHEST,
                     preferred_element_type=F32)
    row = lax.broadcasted_iota(jnp.int32, (8, 128), 0)
    extra = jnp.where(row == 4, jnp.sum(dl, axis=0, keepdims=True), 0.0)
    for q in range(secs):
        buf[0, q, 19] = d_head[0:8]
        buf[0, q, 20] = d_head[8:16]
    spread_g = jnp.dot(dl, hw2[...], precision=lax.Precision.HIGHEST,
                       preferred_element_type=F32) * (1.0 / 64)
    spread_g = spread_g.astype(BF16).astype(F32)

    def tally(k, y, d, sums):
        return (sums[0] + over_pairs(d * zs[k, y]), sums[1] + over_pairs(d))

    def begin(y, sums):
        d = (dsw[5, y].reshape(4, 64, 128) * spread_g[None]).reshape(256, 128)
        du2[y] = d
        return tally(5, y, d, sums)

    sums = lax.fori_loop(0, 8, begin, (zero_sum, zero_sum))
    for k in range(5, -1, -1):
        b, j = k // 2, k % 2
        source = du2 if j == 1 else du1
        c = [k in ks for ks in CHUNKS].index(True)
        at_tile = CHUNKS[c].index(k)
        ends = k == CHUNKS[c][-1]
        r = rs[k]
        dg = both(sums[0]) * r
        db = both(sums[1])
        extra = jnp.where(row == 2 * at_tile, jnp.sum(dg, axis=0, keepdims=True), extra)
        extra = jnp.where(row == 2 * at_tile + 1, jnp.sum(db, axis=0, keepdims=True), extra)
        if ends:
            for q in range(secs):
                buf[c, q, 9 * len(CHUNKS[c])] = extra
            extra = jnp.zeros((8, 128), F32)
        c1 = r * twice(gain[b, j:j + 1, :])
        c2 = c1 * dg * r * (1.0 / 64)

        def settle(y, carry):
            d = (source[y].reshape(4, 64, 128) * c1[None]
                 - zs[k, y].reshape(4, 64, 128) * c2[None])
            if k > 0:
                put(qs, y, d)
            qt[y + 1] = d.reshape(256, 128).T.astype(BF16)
            return carry

        lax.fori_loop(0, 8, settle, 0)

        left = jnp.concatenate(
            [jnp.concatenate([qt[y - a + 2] for y in range(8)], axis=1) for a in range(3)],
            axis=0)
        right = jnp.concatenate([xs[k, y + 1] for y in range(8)], axis=0)
        terms = jnp.dot(left, right, preferred_element_type=F32)
        for a in range(3):
            zero_side = pltpu.roll(terms[a * 128:a * 128 + 64], 64, 1)
            both_sides = zero_side + terms[a * 128 + 64:a * 128 + 128]
            for e in range(3):
                at = e // 2 * 128
                here = both_sides[:, at:at + 128]
                there = pltpu.roll(here, 64, 1)
                first, second = (here, there) if e % 2 == 0 else (there, here)
                for q in range(secs):
                    buf[c, q, at_tile * 9 + a * 3 + e] = jnp.where(
                        low, first[q * 16:q * 16 + 8], second[q * 16 + 8:q * 16 + 16])

        if ends:
            start_a(c)
        if k == 3:
            start_b(0)
        if k == 2:
            start_c(0)

        if j == 1:
            def to_first(y, out, sums):
                d = out * dsw[k - 1, y]
                du1[y] = d
                return tally(k - 1, y, d, sums)

            sums = conv(qs, wb.at[k], to_first, (zero_sum, zero_sum))
            if k == 1:
                start_b(1)
        elif k > 0:
            def to_second(y, out, sums):
                g = (du2[y] + out).astype(BF16).astype(F32)
                d = g * dsw[k - 1, y]
                du2[y] = d
                return tally(k - 1, y, d, sums)

            sums = conv(qs, wb.at[k], to_second, (zero_sum, zero_sum))

    start_c(1)
    start_b(2)
    start_b(3)
    start_c(2)
    start_c(3)
    for c, ks in enumerate(CHUNKS):
        end_c(c)
        for at_tile, k in enumerate(ks):
            rows = [fin[c, at_tile * 9 + t] for t in range(9)]
            conv_out[k, 0:8] = jnp.concatenate([v[:, 0:64] for v in rows], axis=1)
            conv_out[k, 8:16] = jnp.concatenate([v[:, 64:128] for v in rows], axis=1)
            small[2 * k:2 * k + 2] = fin[c, 9 * len(ks)][2 * at_tile:2 * at_tile + 2]
        if c == 0:
            small[12:13] = fin[c, 18][4:5]
            small[16:24] = fin[c, 19]
            small[24:32] = fin[c, 20]
    for b in range(3):
        for d in range(1, secs):
            send_w(b, d).wait_send()
    for c in range(len(CHUNKS)):
        for d in range(1, secs):
            send_a(c, d).wait_send()
        each_dp(lambda d: send_b(c, d).wait_send())
        each_dp(lambda d: send_c(c, d).wait_send())


def all_grads(total, dps, secs, images_in, labels, own, gain, bias, hw, hb):
    vmem = pl.BlockSpec(memory_space=pltpu.VMEM)
    chunks = len(CHUNKS)
    tiles = max(chunk_tiles(c) for c in range(chunks))
    per = -(-tiles // dps)
    hbm = pl.BlockSpec(memory_space=pltpu.HBM)
    dma = pltpu.SemaphoreType.DMA
    return pl.pallas_call(
        functools.partial(kernel, total, dps, secs),
        out_shape=(jax.ShapeDtypeStruct(own.shape, F32),
                   jax.ShapeDtypeStruct((32, 128), F32)),
        in_specs=[hbm, vmem, hbm, vmem, vmem, vmem, vmem],
        out_specs=(vmem, vmem),
        scratch_shapes=[
            pltpu.VMEM((6, 10, 256, 256), BF16),
            pltpu.VMEM((6, 8, 256, 128), F32),
            pltpu.VMEM((6, 8, 256, 128), F32),
            pltpu.VMEM((6, 64, 128), F32),
            pltpu.VMEM((6, 1024, 256), BF16),
            pltpu.VMEM((6, 1024, 256), BF16),
            pltpu.VMEM((10, 256, 256), BF16),
            pltpu.VMEM((10, 128, 256), BF16),
            pltpu.VMEM((8, 256, 128), F32),
            pltpu.VMEM((8, 256, 128), F32),
            pltpu.VMEM((128, 128), F32),
            pltpu.VMEM((8, 128), jnp.int32),
            pltpu.VMEM((secs,) + own.shape, BF16),
            pltpu.VMEM((chunks, secs, tiles, 8, 128), F32),
            pltpu.VMEM((chunks, secs - 1, tiles, 8, 128), F32),
            pltpu.VMEM((chunks, per * dps, 8, 128), F32),
            pltpu.VMEM((chunks, dps - 1, per, 8, 128), F32),
            pltpu.VMEM((chunks, per * dps, 8, 128), F32),
            pltpu.VMEM(images_in.shape, BF16),
            pltpu.VMEM(own.shape, F32),
            dma((2,)),
            dma((3, secs - 1)), dma((3, secs - 1)),
            dma((chunks, secs - 1)), dma((chunks, secs - 1)),
            dma((chunks, dps - 1)), dma((chunks, dps - 1)),
            dma((chunks, dps - 1)), dma((chunks, dps - 1)),
        ],
        compiler_params=pltpu.CompilerParams(
            vmem_limit_bytes=63 * 1024 * 1024 + 768 * 1024, collective_id=0, has_side_effects=True),
    )(images_in, labels, own, gain, bias, hw, hb)


def per_device(images_in, labels, conv_weight, frn_gain, frn_bias, head_weight, head_bias):
    images = images_in.shape[0]
    dps, secs = lax.axis_size("dp"), lax.axis_size("section")
    blocks, convs, depth, share = conv_weight.shape
    own = jnp.swapaxes(conv_weight, 2, 3).reshape(blocks * convs, share, depth)
    owned, small = all_grads(images * dps * secs, dps, secs, images_in,
                             labels.reshape(1, images), own, frn_gain,
                             frn_bias, head_weight.T, head_bias.reshape(1, -1))
    classes = head_bias.shape[0]
    params = jnp.stack([frn_gain, frn_bias], axis=2)
    return (
        jnp.swapaxes(owned.reshape(blocks, convs, share, depth), 2, 3)
        + prior_precision * conv_weight,
        small[0:12, 0:64].reshape(params.shape)
        + prior_precision * params,
        small[16:16 + classes, 0:64].T + prior_precision * head_weight,
        small[12, 0:classes] + prior_precision * head_bias,
    )


def solution(mesh):
    return jax.shard_map(
        per_device,
        mesh=mesh,
        in_specs=(
            P(("dp", "section"), None),
            P(("dp", "section")),
            P(None, None, None, "section"),
            P(),
            P(),
            P(),
            P(),
        ),
        out_specs=(P(None, None, None, "section"), P(), P(), P()),
        check_vma=False,
    )
```
